1024 devices in a mesh: fsdp: 256 (over y_lo, x, z), rep: 4 (over y_hi, core).
Axes of the slice: x: 4, y: 8 (y_hi: 2, y_lo: 4; y = y_hi * 4 + y_lo), z: 16, core: 2. Of those that a mesh axis runs over, the one named last changes fastest.
Arguments:
- tokens: bfloat16 [131072, 320], P(('fsdp', 'rep')), may hold values from -6 to 6
- weight: bfloat16 [16384, 6656], P('fsdp'), may hold values from -0.3125 to 0.3125
- cotangent: bfloat16 [131072, 6656], P(('fsdp', 'rep')), may hold values from -0.59765625 to 0.59765625
Outputs:
- token_grad: bfloat16 [131072, 320], P(('fsdp', 'rep'))
- weight_grad: bfloat16 [16384, 6656], P('fsdp')
The draws below stay inside these ranges and needn't reach their ends.
All inputs are finite; a program needn't handle non-finite values.
Results may differ from the reference program's by a relative error of at most 0.013.
Values may be sent and summed in bfloat16 or wider, within the bound.
No kernel may reach another device: no remote copies, remote signals or barrier semaphores. Data moves between devices by JAX's collectives and lax.ppermute only.
A program may use at most 32 MiB of HBM per device.

```python
import jax
import jax.numpy as jnp
from jax import lax

F = 6656
DS = 64
HOPS = 2
TOK_DEV = 128
SPAN = 5
D = 16384
TOKENS = 131072
N_FSDP = 256
N_REP = 4


def block_levels(key, extent, pieces, low, largest):
    loudness, own = 1.0, jax.random.fold_in(key, 6)
    for dim, shards_of in pieces:
        steps = jnp.exp(jax.random.uniform(jax.random.fold_in(own, dim), (shards_of,), jnp.float32, low / len(pieces), largest / len(pieces)))
        loudness = loudness * jnp.repeat(steps, extent[dim] // shards_of).reshape([-1 if axis == dim else 1 for axis in range(len(extent))])
    return loudness


def bell_draw(own_key, extent, deviation, reach, split=(), kind=jnp.bfloat16):
    array = jax.random.normal(own_key, extent, jnp.float32) * deviation
    if len(split) > 0:
        array = block_levels(own_key, extent, split, -0.22, 0.18) * array
    return jnp.clip(array, min=-reach, max=reach).astype(kind)


def setup_inputs(seed: int = 0) -> dict:
    key_of = jax.random.split(jax.random.key(seed), 4)
    return {
        "tokens": bell_draw(key_of[0], (TOKENS, SPAN * DS), 1.0, 6.0, ((0, 1024),)),
        "weight": bell_draw(key_of[1], (D, F), (SPAN * DS) ** -0.5, 0.3125, ((0, 256),)),
        "cotangent": bell_draw(key_of[2], (TOKENS, F), 0.1, 0.59765625, ((0, 1024),)),
    }


def reference(tokens, weight, cotangent):
    count = N_FSDP
    token_blocks = tokens.reshape(count, N_REP * TOK_DEV, SPAN * DS)
    weight_blocks = weight.reshape(count, DS, F)
    upstream_blocks = cotangent.reshape(count, N_REP * TOK_DEV, F)
    offsets = jnp.arange(SPAN, dtype=jnp.int32) - HOPS
    devices = jnp.arange(count, dtype=jnp.int32)

    def backward_one(device):
        local_rows = lax.dynamic_index_in_dim(token_blocks, device, 0, keepdims=False)
        local_upstream = lax.dynamic_index_in_dim(upstream_blocks, device, 0, keepdims=False)
        chosen = jnp.take(weight_blocks, (device + offsets) % count, axis=0).reshape(SPAN * DS, F)
        preact = jnp.dot(local_rows, chosen, preferred_element_type=jnp.float32)
        logistic = jax.nn.sigmoid(preact)
        slope = (local_upstream.astype(jnp.float32) * logistic * (1.0 + preact * (1.0 - logistic))).astype(jnp.bfloat16)
        input_grad = lax.dot_general(slope, chosen, (((1,), (1,)), ((), ())), preferred_element_type=jnp.float32)
        return (slope, input_grad.astype(jnp.bfloat16))
    slopes, input_grads = lax.map(backward_one, devices)
    token_grad = input_grads.reshape(count * N_REP * TOK_DEV, SPAN * DS)

    def owner_grad(owner):
        summed = jnp.zeros((N_REP, DS, F), jnp.float32)
        for position in range(SPAN):
            source = ((owner - position + HOPS) % count).astype(jnp.int32)
            slab = lax.dynamic_index_in_dim(token_blocks, source, 0, keepdims=False)[:, position * DS:(position + 1) * DS]
            slab = slab.reshape(N_REP, TOK_DEV, DS).astype(jnp.float32)
            upstream = lax.dynamic_index_in_dim(slopes, source, 0, keepdims=False).reshape(N_REP, TOK_DEV, F).astype(jnp.float32)
            partial_term = lax.optimization_barrier(jnp.einsum('rtd,rtf->rdf', slab, upstream).astype(jnp.bfloat16))
            summed = summed + partial_term.astype(jnp.float32)
        per_group = lax.optimization_barrier(summed.astype(jnp.bfloat16)).astype(jnp.float32)
        return lax.optimization_barrier(jnp.sum(per_group, axis=0)).astype(jnp.bfloat16)
    weight_grad = lax.map(owner_grad, devices).reshape(count * DS, F)
    return (token_grad, weight_grad)
```

```python
import jax
import jax.numpy as jnp
from jax import lax
from jax.experimental import pallas as pl
from jax.experimental.pallas import tpu as pltpu
from jax.sharding import PartitionSpec as P

AXES = ("fsdp", "rep")
SPAN = 5


def _sub(width):
    cuts = list(range(0, width, 256)) + [width]
    return list(zip(cuts[:-1], cuts[1:]))


def gate_kernel(core, tok_t, w_a2, w_a1, w_0, w_b1, w_b2, cot_a, cot_b,
                p_a2, p_a1, p_0, p_b1, p_b2, tg, slope_s):
    del core
    tt = tok_t[...]
    tok = tt.T
    half = cot_a.shape[0]
    rows = w_0.shape[0]
    blocks = (w_a2, w_a1, w_0, w_b1, w_b2)
    outs = (p_a2, p_a1, p_0, p_b1, p_b2)
    for lo, hi in _sub(w_0.shape[1]):
        band = jnp.concatenate([w[:, lo:hi] for w in blocks], axis=0)
        pre = jnp.dot(tok, band, preferred_element_type=jnp.float32)
        s = 0.5 * jnp.tanh(0.5 * pre) + 0.5
        d = s * (1.0 + pre * (1.0 - s))
        up = jnp.concatenate([cot_a[:, lo:hi], cot_b[:, lo:hi]], axis=0)
        slope = (up.astype(jnp.float32) * d).astype(jnp.bfloat16)
        slope_s[:, lo:hi] = slope
        part = jnp.dot(tt, slope, preferred_element_type=jnp.float32)
        for k in range(SPAN):
            outs[k][:, lo:hi] = part[k * rows:(k + 1) * rows].astype(outs[k].dtype)
    band = jnp.concatenate([w[...] for w in blocks], axis=0)
    grad = lax.dot_general(band, slope_s[...], (((1,), (1,)), ((), ())),
                           preferred_element_type=jnp.float32)

    @pl.when(pl.program_id(0) == 0)
    def _():
        tg[...] = grad

    @pl.when(pl.program_id(0) > 0)
    def _():
        tg[...] += grad


def gate(core, tok_t, blocks, cotangent, cot_other, steps):
    shard, cols = blocks[0].shape
    width, both = tok_t.shape
    bc = cols // steps
    w_spec = pl.BlockSpec((shard, bc), lambda j, c: (0, j))
    c_own = pl.BlockSpec((both // 2, bc), lambda j, c: (0, c[0] * steps + j))
    c_oth = pl.BlockSpec((both // 2, bc), lambda j, c: (0, j))
    whole = pl.BlockSpec((width, both), lambda j, c: (0, 0))
    return pl.pallas_call(
        gate_kernel,
        grid_spec=pltpu.PrefetchScalarGridSpec(
            num_scalar_prefetch=1,
            grid=(steps,),
            in_specs=[whole] + [w_spec] * SPAN + [c_own, c_oth],
            out_specs=[w_spec] * SPAN + [whole],
            scratch_shapes=[pltpu.VMEM((both, bc), jnp.bfloat16)],
        ),
        out_shape=[jax.ShapeDtypeStruct((shard, cols), jnp.bfloat16)] * SPAN
        + [jax.ShapeDtypeStruct((width, both), jnp.float32)],
        compiler_params=pltpu.CompilerParams(vmem_limit_bytes=32 * 1024 * 1024),
        cost_estimate=pl.CostEstimate(
            flops=6 * width * both * cols, bytes_accessed=6 * 1024 * 1024, transcendentals=both * cols
        ),
    )(core, tok_t, *blocks, cotangent, cot_other)


def solution(mesh):
    n_f, n_r = mesh.shape["fsdp"], mesh.shape["rep"]

    def pairs(move):
        out = []
        for p in range(n_f):
            for r in range(n_r):
                q, t = move(p, r)
                out.append((p * n_r + r, (q % n_f) * n_r + t))
        return out

    ring_a = pairs(lambda p, r: (p + (1 if r % 2 == 0 else -1), r))
    ring_b = pairs(lambda p, r: (p + (-1 if r % 2 == 0 else 1), r))
    swap_core = pairs(lambda p, r: (p, r ^ 1))
    swap_far = pairs(lambda p, r: (p, r ^ 2))
    core_groups = [[g, g + 1] for g in range(0, n_r, 2)]

    def on_device(tokens, weight, cotangent):
        core = lax.axis_index("rep") % 2
        shard, f = weight.shape
        cols = f // 2
        rows = tokens.shape[0]

        def flip(t):
            back = t.reshape(SPAN, shard, t.shape[1])[::-1].reshape(t.shape)
            return jnp.where(core == 0, t, back)

        send = lambda v, how: lax.ppermute(v, AXES, how)
        w_0 = lax.dynamic_slice(weight, (0, core * cols), (shard, cols))
        w_a1 = send(w_0, ring_a)
        w_b1 = send(w_0, ring_b)
        w_a2 = send(w_a1, ring_a)
        w_b2 = send(w_b1, ring_b)
        cot_out = lax.dynamic_slice(cotangent, (0, (1 - core) * cols), (rows, cols))
        cot_other = send(cot_out, swap_core)
        tok_own = tokens.T
        tok_other = send(tok_own, swap_core)
        tok_t = flip(jnp.concatenate([tok_own, tok_other], axis=1))
        p_a2, p_a1, p_0, p_b1, p_b2, tg = gate(
            core.reshape(1).astype(jnp.int32), tok_t, (w_a2, w_a1, w_0, w_b1, w_b2),
            cotangent, cot_other, 2)
        f32 = lambda v: v.astype(jnp.float32)
        g_a = send(p_b2, ring_a)
        g_b = send(p_a2, ring_b)
        g_a = send((f32(g_a) + f32(p_b1)).astype(jnp.bfloat16), ring_a)
        g_b = send((f32(g_b) + f32(p_a1)).astype(jnp.bfloat16), ring_b)
        mine = (f32(p_0) + f32(g_a) + f32(g_b)).astype(jnp.bfloat16)
        far = send(mine, swap_far)
        half = (f32(mine) + f32(far)).astype(jnp.bfloat16)
        weight_grad = lax.all_gather(half, "rep", axis=1, tiled=True, axis_index_groups=core_groups)
        tg = flip(tg)
        tg_other = send(tg[:, rows:], swap_core)
        token_grad = (tg[:, :rows] + tg_other).astype(jnp.bfloat16).T
        return (token_grad, weight_grad)

    return jax.shard_map(
        on_device,
        mesh=mesh,
        in_specs=(P(AXES, None), P("fsdp", None), P(AXES, None)),
        out_specs=(P(AXES, None), P("fsdp", None)),
        check_vma=False,
    )
```

```python
import jax
import jax.numpy as jnp
from jax import lax
from jax.experimental import pallas as pl
from jax.experimental.pallas import tpu as pltpu
from jax.sharding import PartitionSpec as P

AXES = ("fsdp", "rep")
HOPS = 2
SPAN = 5
MIB = 1024 * 1024


def _band(near, far, w_own):
    n = near[0].shape[0] // 2
    below = [v[:n] for v in far] + [v[:n] for v in near]
    above = [v[n:] for v in near] + [v[n:] for v in far]
    return jnp.concatenate(below + [w_own[...]] + above, axis=0)


def slope_kernel(with_own, core, tok_a, tok_b, n0, n1, f0, f1, w_own, cot_a, cot_b, p_two, p_one, *rest):
    slope_out, tok_s = rest[-2:]
    rows = w_own.shape[0]
    half = tok_a.shape[1]
    tok_s[:, :half] = tok_a[...]
    tok_s[:, half:] = tok_b[...]
    pre = jnp.dot(tok_s[...].T, _band((n0, n1), (f0, f1), w_own), preferred_element_type=jnp.float32)
    s = 0.5 * jnp.tanh(0.5 * pre) + 0.5
    d = s * (1.0 + pre * (1.0 - s))
    up = jnp.concatenate([cot_a[...], cot_b[...]], axis=0)
    slope = (up.astype(jnp.float32) * d).astype(jnp.bfloat16)
    slope_out[...] = slope[:half]
    two = pl.multiple_of(jnp.where(core[0] == 0, SPAN - 1, 0) * rows, rows)
    one = pl.multiple_of(jnp.where(core[0] == 0, SPAN - 2, 1) * rows, rows)
    blocks = [tok_s[pl.ds(two, rows)], tok_s[pl.ds(one, rows)]]
    if with_own:
        blocks.append(tok_s[HOPS * rows:(HOPS + 1) * rows])
    part = jnp.dot(jnp.concatenate(blocks, axis=0), slope, preferred_element_type=jnp.float32)
    p_two[...] = part[:rows].astype(jnp.bfloat16)
    p_one[...] = part[rows:2 * rows].astype(jnp.bfloat16)
    if with_own:
        rest[0][...] = part[2 * rows:].astype(jnp.bfloat16)


def grad_kernel(core, n0, n1, f0, f1, w_own, s_first, s_second, tg):
    cols = s_first.shape[1]

    def one(first, second):
        band = _band((n0, n1), (f0, f1), w_own)
        total = jnp.zeros(tg.shape, jnp.float32)
        for k, slope in enumerate((first, second)):
            total += lax.dot_general(band[:, k * cols:(k + 1) * cols], slope[...], (((1,), (1,)), ((), ())),
                                     preferred_element_type=jnp.float32)
        tg[...] = total.astype(tg.dtype)

    @pl.when(core[0] == 0)
    def _():
        one(s_second, s_first)

    @pl.when(core[0] != 0)
    def _():
        one(s_first, s_second)


def slopes(core, tok_a, tok_b, pairs, weight, cot_a, cot_b, own_cols):
    width, rows = tok_a.shape
    shard, cols = weight.shape[0], weight.shape[1] // 2
    where = (lambda i, c: (0, c[0])) if own_cols else (lambda i, c: (0, 1 - c[0]))
    whole = lambda v: pl.BlockSpec(v.shape, lambda i, c: (0, 0))
    col = lambda v: pl.BlockSpec((v.shape[0], cols), where)
    out = lambda r: pl.BlockSpec((r, cols), lambda i, c: (0, 0))
    heights = [shard] * (3 if own_cols else 2) + [rows]
    return pl.pallas_call(
        lambda *refs: slope_kernel(own_cols, *refs),
        grid_spec=pltpu.PrefetchScalarGridSpec(
            num_scalar_prefetch=1,
            grid=(1,),
            in_specs=[whole(tok_a), whole(tok_b)] + [col(v) for v in pairs] + [col(weight), col(cot_a), col(cot_b)],
            out_specs=[out(r) for r in heights],
            scratch_shapes=[pltpu.VMEM((width, 2 * rows), jnp.bfloat16)],
        ),
        out_shape=[jax.ShapeDtypeStruct((r, cols), jnp.bfloat16) for r in heights],
        compiler_params=pltpu.CompilerParams(vmem_limit_bytes=40 * MIB),
        cost_estimate=pl.CostEstimate(flops=7 * width * rows * cols, bytes_accessed=6 * MIB,
                                      transcendentals=2 * rows * cols),
    )(core, tok_a, tok_b, *pairs, weight, cot_a, cot_b)


def token_gradient(core, pairs, weight, first, second, width):
    rows = first.shape[0]
    whole = lambda v: pl.BlockSpec(v.shape, lambda i, c: (0, 0))
    return pl.pallas_call(
        grad_kernel,
        grid_spec=pltpu.PrefetchScalarGridSpec(
            num_scalar_prefetch=1,
            grid=(1,),
            in_specs=[whole(v) for v in (*pairs, weight, first, second)],
            out_specs=pl.BlockSpec((width, rows), lambda i, c: (0, 0)),
        ),
        out_shape=jax.ShapeDtypeStruct((width, rows), jnp.bfloat16),
        compiler_params=pltpu.CompilerParams(vmem_limit_bytes=40 * MIB),
        cost_estimate=pl.CostEstimate(flops=4 * width * rows * first.shape[1], bytes_accessed=6 * MIB, transcendentals=0),
    )(core, *pairs, weight, first, second)


def solution(mesh):
    n_f, n_r = mesh.shape["fsdp"], mesh.shape["rep"]

    def pairs_of(move):
        out = []
        for p in range(n_f):
            for r in range(n_r):
                q, t = move(p, r)
                if q != q % n_f:
                    t ^= 2
                out.append((p * n_r + r, (q % n_f) * n_r + t))
        return out

    ring = pairs_of(lambda p, r: (p + (1 if r % 2 == 0 else -1), r))
    swap_core = pairs_of(lambda p, r: (p, r ^ 1))
    swap_far = pairs_of(lambda p, r: (p, r ^ 2))
    core_groups = [[g, g + 1] for g in range(0, n_r, 2)]

    def on_device(tokens, weight, cotangent):
        core = lax.axis_index("rep") % 2
        half = weight.shape[0] // 2

        def send(v, how=ring):
            return lax.ppermute(v, AXES, how)

        def gather(v, axis):
            return lax.all_gather(v, "rep", axis=axis, tiled=True, axis_index_groups=core_groups)

        f32 = lambda v: v.astype(jnp.float32)
        b16 = lambda v: v.astype(jnp.bfloat16)
        near = [send(weight[:half]), send(weight[half:])]
        far = [send(v) for v in near]
        cot_b = send(cotangent, swap_core)
        tok_a = tokens.T
        tok_b = send(tok_a, swap_core)
        pairs = [gather(v, 0) for v in near + far]
        which = core.reshape(1).astype(jnp.int32)
        two, one, slope_1 = slopes(which, tok_a, tok_b, pairs, weight, cotangent, cot_b, False)
        g_1 = send(two)
        two_2, one_2, own, slope_2 = slopes(which, tok_a, tok_b, pairs, weight, cotangent, cot_b, True)
        g_2 = send(two_2)
        g_1 = send(b16(f32(g_1) + f32(one)))
        g_2 = send(b16(f32(g_2) + f32(one_2)))
        got = send(g_1, swap_core)
        mine = b16(f32(own) + f32(g_2) + f32(got))
        other = send(mine, swap_far)
        weight_grad = gather(b16(f32(mine) + f32(other)), 1)
        token_grad = token_gradient(which, pairs, weight, slope_1, slope_2, tokens.shape[1]).T
        return (token_grad, weight_grad)

    return jax.shard_map(
        on_device,
        mesh=mesh,
        in_specs=(P(AXES, None), P("fsdp", None), P(AXES, None)),
        out_specs=(P(AXES, None), P("fsdp", None)),
        check_vma=False,
    )
```

```python
import jax
import jax.numpy as jnp
from jax import lax
from jax.experimental import pallas as pl
from jax.experimental.pallas import tpu as pltpu
from jax.sharding import PartitionSpec as P

AXES = ("fsdp", "rep")
HOPS = 2
LINE = 16
SPAN = 5
MIB = 1024 * 1024


def _band(near, far, w_own):
    n = near[0].shape[0] // 2
    below = [v[:n] for v in far] + [v[:n] for v in near]
    above = [v[n:] for v in near] + [v[n:] for v in far]
    return jnp.concatenate(below + [w_own[...]] + above, axis=0)


def slope_kernel(with_own, core, tok_a, tok_b, n0, n1, f0, f1, w_own, cot_a, cot_b, p_two, p_one, *rest):
    slope_out, tok_s = rest[-2:]
    rows = w_own.shape[0]
    half = tok_a.shape[1]
    tok_s[:, :half] = tok_a[...]
    tok_s[:, half:] = tok_b[...]
    pre = jnp.dot(tok_s[...].T, _band((n0, n1), (f0, f1), w_own), preferred_element_type=jnp.float32)
    s = 0.5 * jnp.tanh(0.5 * pre) + 0.5
    d = s * (1.0 + pre * (1.0 - s))
    up = jnp.concatenate([cot_a[...], cot_b[...]], axis=0)
    slope = (up.astype(jnp.float32) * d).astype(jnp.bfloat16)
    slope_out[...] = slope[:half]
    two = pl.multiple_of(jnp.where(core[0] == 0, SPAN - 1, 0) * rows, rows)
    one = pl.multiple_of(jnp.where(core[0] == 0, SPAN - 2, 1) * rows, rows)
    blocks = [tok_s[pl.ds(two, rows)], tok_s[pl.ds(one, rows)]]
    if with_own:
        blocks.append(tok_s[HOPS * rows:(HOPS + 1) * rows])
    part = jnp.dot(jnp.concatenate(blocks, axis=0), slope, preferred_element_type=jnp.float32)
    p_two[...] = part[:rows].astype(jnp.bfloat16)
    p_one[...] = part[rows:2 * rows].astype(jnp.bfloat16)
    if with_own:
        rest[0][...] = part[2 * rows:].astype(jnp.bfloat16)


def grad_kernel(core, n0, n1, f0, f1, w_own, s_first, s_second, tg):
    cols = s_first.shape[1]

    def one(first, second):
        band = _band((n0, n1), (f0, f1), w_own)
        total = jnp.zeros(tg.shape, jnp.float32)
        for k, slope in enumerate((first, second)):
            total += lax.dot_general(band[:, k * cols:(k + 1) * cols], slope[...], (((1,), (1,)), ((), ())),
                                     preferred_element_type=jnp.float32)
        tg[...] = total.astype(tg.dtype)

    @pl.when(core[0] == 0)
    def _():
        one(s_second, s_first)

    @pl.when(core[0] != 0)
    def _():
        one(s_first, s_second)


def slopes(core, tok_a, tok_b, pairs, weight, cot_a, cot_b, own_cols):
    width, rows = tok_a.shape
    shard, cols = weight.shape[0], weight.shape[1] // 2
    where = (lambda i, c: (0, c[0])) if own_cols else (lambda i, c: (0, 1 - c[0]))
    whole = lambda v: pl.BlockSpec(v.shape, lambda i, c: (0, 0))
    col = lambda v: pl.BlockSpec((v.shape[0], cols), where)
    out = lambda r: pl.BlockSpec((r, cols), lambda i, c: (0, 0))
    heights = [shard] * (3 if own_cols else 2) + [rows]
    return pl.pallas_call(
        lambda *refs: slope_kernel(own_cols, *refs),
        grid_spec=pltpu.PrefetchScalarGridSpec(
            num_scalar_prefetch=1,
            grid=(1,),
            in_specs=[whole(tok_a), whole(tok_b)] + [col(v) for v in pairs] + [col(weight), col(cot_a), col(cot_b)],
            out_specs=[out(r) for r in heights],
            scratch_shapes=[pltpu.VMEM((width, 2 * rows), jnp.bfloat16)],
        ),
        out_shape=[jax.ShapeDtypeStruct((r, cols), jnp.bfloat16) for r in heights],
        compiler_params=pltpu.CompilerParams(vmem_limit_bytes=40 * MIB),
        cost_estimate=pl.CostEstimate(flops=7 * width * rows * cols, bytes_accessed=6 * MIB,
                                      transcendentals=2 * rows * cols),
    )(core, tok_a, tok_b, *pairs, weight, cot_a, cot_b)


def token_gradient(core, pairs, weight, first, second, width):
    rows = first.shape[0]
    whole = lambda v: pl.BlockSpec(v.shape, lambda i, c: (0, 0))
    return pl.pallas_call(
        grad_kernel,
        grid_spec=pltpu.PrefetchScalarGridSpec(
            num_scalar_prefetch=1,
            grid=(1,),
            in_specs=[whole(v) for v in (*pairs, weight, first, second)],
            out_specs=pl.BlockSpec((width, rows), lambda i, c: (0, 0)),
        ),
        out_shape=jax.ShapeDtypeStruct((width, rows), jnp.bfloat16),
        compiler_params=pltpu.CompilerParams(vmem_limit_bytes=40 * MIB),
        cost_estimate=pl.CostEstimate(flops=4 * width * rows * first.shape[1], bytes_accessed=6 * MIB, transcendentals=0),
    )(core, *pairs, weight, first, second)


def solution(mesh):
    n_f, n_r = mesh.shape["fsdp"], mesh.shape["rep"]

    def pairs_of(move):
        out = []
        for p in range(n_f):
            for r in range(n_r):
                q, t = move(p, r)
                if q != q % n_f:
                    t ^= 2
                out.append((p * n_r + r, (q % n_f) * n_r + t))
        return out

    ring = pairs_of(lambda p, r: (p + (1 if r % 2 == 0 else -1), r))
    crosses = lambda pair: (pair[0] // n_r) // LINE != (pair[1] // n_r) // LINE
    inner = [pair for pair in ring if not crosses(pair)]
    outer = [pair for pair in ring if crosses(pair)]
    swap_core = pairs_of(lambda p, r: (p, r ^ 1))
    swap_far = pairs_of(lambda p, r: (p, r ^ 2))
    core_groups = [[g, g + 1] for g in range(0, n_r, 2)]

    def on_device(tokens, weight, cotangent):
        core = lax.axis_index("rep") % 2
        half = weight.shape[0] // 2

        def send(v, how):
            return lax.ppermute(v, AXES, how)

        def gather(v, axis):
            return lax.all_gather(v, "rep", axis=axis, tiled=True, axis_index_groups=core_groups)

        f32 = lambda v: v.astype(jnp.float32)
        b16 = lambda v: v.astype(jnp.bfloat16)
        step_in = send(weight, inner)
        step_out = send(weight, outer)
        far_out = send(step_in, outer)
        step = step_in + step_out
        near = [step[:half], step[half:]]
        far = [send(v, inner) for v in near]
        far = [far[0] + far_out[:half], far[1] + far_out[half:]]
        cot_b = send(cotangent, swap_core)
        tok_a = tokens.T
        tok_b = send(tok_a, swap_core)
        pairs = [gather(v, 0) for v in near + far]
        which = core.reshape(1).astype(jnp.int32)
        two, one, slope_1 = slopes(which, tok_a, tok_b, pairs, weight, cotangent, cot_b, False)
        g_1 = send(two, ring)
        two_2, one_2, own, slope_2 = slopes(which, tok_a, tok_b, pairs, weight, cotangent, cot_b, True)
        g_2 = send(two_2, ring)
        g_1 = send(b16(f32(g_1) + f32(one)), ring)
        g_2 = send(b16(f32(g_2) + f32(one_2)), ring)
        got = send(g_1, swap_core)
        mine = b16(f32(own) + f32(g_2) + f32(got))
        other = send(mine, swap_far)
        weight_grad = gather(b16(f32(mine) + f32(other)), 1)
        token_grad = token_gradient(which, pairs, weight, slope_1, slope_2, tokens.shape[1]).T
        return (token_grad, weight_grad)

    return jax.shard_map(
        on_device,
        mesh=mesh,
        in_specs=(P(AXES, None), P("fsdp", None), P(AXES, None)),
        out_specs=(P(AXES, None), P("fsdp", None)),
        check_vma=False,
    )
```

```python
import jax
import jax.numpy as jnp
from jax import lax
from jax.experimental import pallas as pl
from jax.experimental.pallas import tpu as pltpu
from jax.sharding import PartitionSpec as P

AXES = ("fsdp", "rep")
HOPS = 2
LINE = 16
SPAN = 5
MIB = 1024 * 1024


def _band(near, far, w_own):
    n = near[0].shape[0] // 2
    below = [v[:n] for v in far] + [v[:n] for v in near]
    above = [v[n:] for v in near] + [v[n:] for v in far]
    return jnp.concatenate(below + [w_own[...]] + above, axis=0)


def slope_kernel(with_own, core, tok_a, tok_b, n0, n1, f0, f1, w_own, cot_a, cot_b, p_two, p_one, *rest):
    slope_out, tok_s = rest[-2:]
    rows = w_own.shape[0]
    half = tok_a.shape[1]
    tok_s[:, :half] = tok_a[...]
    tok_s[:, half:] = tok_b[...]
    pre = jnp.dot(tok_s[...].T, _band((n0, n1), (f0, f1), w_own), preferred_element_type=jnp.float32)
    s = 0.5 * jnp.tanh(0.5 * pre) + 0.5
    d = s * (1.0 + pre * (1.0 - s))
    up = jnp.concatenate([cot_a[...], cot_b[...]], axis=0)
    slope = (up.astype(jnp.float32) * d).astype(jnp.bfloat16)
    slope_out[...] = slope[:half]
    two = pl.multiple_of(jnp.where(core[0] == 0, SPAN - 1, 0) * rows, rows)
    one = pl.multiple_of(jnp.where(core[0] == 0, SPAN - 2, 1) * rows, rows)
    blocks = [tok_s[pl.ds(two, rows)], tok_s[pl.ds(one, rows)]]
    if with_own:
        blocks.append(tok_s[HOPS * rows:(HOPS + 1) * rows])
    part = jnp.dot(jnp.concatenate(blocks, axis=0), slope, preferred_element_type=jnp.float32)
    p_two[...] = part[:rows].astype(jnp.bfloat16)
    p_one[...] = part[rows:2 * rows].astype(jnp.bfloat16)
    if with_own:
        rest[0][...] = part[2 * rows:].astype(jnp.bfloat16)


def grad_kernel(core, n0, n1, f0, f1, w_own, s_first, s_second, tg):
    cols = s_first.shape[1]

    def one(first, second):
        band = _band((n0, n1), (f0, f1), w_own)
        total = jnp.zeros(tg.shape, jnp.float32)
        for k, slope in enumerate((first, second)):
            total += lax.dot_general(band[:, k * cols:(k + 1) * cols], slope[...], (((1,), (1,)), ((), ())),
                                     preferred_element_type=jnp.float32)
        tg[...] = total.astype(tg.dtype)

    @pl.when(core[0] == 0)
    def _():
        one(s_second, s_first)

    @pl.when(core[0] != 0)
    def _():
        one(s_first, s_second)


def slopes(core, tok_a, tok_b, pairs, weight, cot_a, cot_b, own_cols):
    width, rows = tok_a.shape
    shard, cols = weight.shape[0], weight.shape[1] // 2
    where = (lambda i, c: (0, c[0])) if own_cols else (lambda i, c: (0, 1 - c[0]))
    whole = lambda v: pl.BlockSpec(v.shape, lambda i, c: (0, 0))
    col = lambda v: pl.BlockSpec((v.shape[0], cols), where)
    out = lambda r: pl.BlockSpec((r, cols), lambda i, c: (0, 0))
    heights = [shard] * (3 if own_cols else 2) + [rows]
    return pl.pallas_call(
        lambda *refs: slope_kernel(own_cols, *refs),
        grid_spec=pltpu.PrefetchScalarGridSpec(
            num_scalar_prefetch=1,
            grid=(1,),
            in_specs=[whole(tok_a), whole(tok_b)] + [col(v) for v in pairs] + [col(weight), col(cot_a), col(cot_b)],
            out_specs=[out(r) for r in heights],
            scratch_shapes=[pltpu.VMEM((width, 2 * rows), jnp.bfloat16)],
        ),
        out_shape=[jax.ShapeDtypeStruct((r, cols), jnp.bfloat16) for r in heights],
        compiler_params=pltpu.CompilerParams(vmem_limit_bytes=40 * MIB),
        cost_estimate=pl.CostEstimate(flops=7 * width * rows * cols, bytes_accessed=6 * MIB,
                                      transcendentals=2 * rows * cols),
    )(core, tok_a, tok_b, *pairs, weight, cot_a, cot_b)


def token_gradient(core, pairs, weight, first, second, width):
    rows = first.shape[0]
    whole = lambda v: pl.BlockSpec(v.shape, lambda i, c: (0, 0))
    return pl.pallas_call(
        grad_kernel,
        grid_spec=pltpu.PrefetchScalarGridSpec(
            num_scalar_prefetch=1,
            grid=(1,),
            in_specs=[whole(v) for v in (*pairs, weight, first, second)],
            out_specs=pl.BlockSpec((width, rows), lambda i, c: (0, 0)),
        ),
        out_shape=jax.ShapeDtypeStruct((width, rows), jnp.bfloat16),
        compiler_params=pltpu.CompilerParams(vmem_limit_bytes=40 * MIB),
        cost_estimate=pl.CostEstimate(flops=4 * width * rows * first.shape[1], bytes_accessed=6 * MIB, transcendentals=0),
    )(core, *pairs, weight, first, second)


def solution(mesh):
    n_f, n_r = mesh.shape["fsdp"], mesh.shape["rep"]

    def pairs_of(move):
        out = []
        for p in range(n_f):
            for r in range(n_r):
                q, t = move(p, r)
                if q != q % n_f:
                    t ^= 2
                out.append((p * n_r + r, (q % n_f) * n_r + t))
        return out

    ring = pairs_of(lambda p, r: (p + (1 if r % 2 == 0 else -1), r))
    crosses = lambda pair: (pair[0] // n_r) // LINE != (pair[1] // n_r) // LINE
    inner = [pair for pair in ring if not crosses(pair)]
    outer = [pair for pair in ring if crosses(pair)]
    swap_core = pairs_of(lambda p, r: (p, r ^ 1))
    far_groups = [[g, g + 2] for g in range(2)]
    core_groups = [[g, g + 1] for g in range(0, n_r, 2)]

    def on_device(tokens, weight, cotangent):
        core = lax.axis_index("rep") % 2
        half = weight.shape[0] // 2

        def send(v, how):
            return lax.ppermute(v, AXES, how)

        def gather(v, axis):
            return lax.all_gather(v, "rep", axis=axis, tiled=True, axis_index_groups=core_groups)

        f32 = lambda v: v.astype(jnp.float32)
        b16 = lambda v: v.astype(jnp.bfloat16)
        step_in = send(weight, inner)
        step_out = send(weight, outer)
        far_out = send(step_in, outer)
        step = step_in + step_out
        near = [step[:half], step[half:]]
        far = [send(v, inner) for v in near]
        far = [far[0] + far_out[:half], far[1] + far_out[half:]]
        cot_b = send(cotangent, swap_core)
        tok_a = tokens.T
        tok_b = send(tok_a, swap_core)
        pairs = [gather(v, 0) for v in near + far]
        which = core.reshape(1).astype(jnp.int32)
        two, one, slope_1 = slopes(which, tok_a, tok_b, pairs, weight, cotangent, cot_b, False)
        g_1 = send(two, ring)
        two_2, one_2, own, slope_2 = slopes(which, tok_a, tok_b, pairs, weight, cotangent, cot_b, True)
        g_2 = send(two_2, ring)
        g_1 = send(b16(f32(g_1) + f32(one)), ring)
        g_2 = send(b16(f32(g_2) + f32(one_2)), ring)
        got = send(g_1, swap_core)
        mine = b16(f32(own) + f32(g_2) + f32(got))
        both = lax.all_gather(mine, "rep", axis=0, tiled=True, axis_index_groups=far_groups)
        rows = weight.shape[0]
        weight_grad = gather(b16(f32(both[:rows]) + f32(both[rows:])), 1)
        token_grad = token_gradient(which, pairs, weight, slope_1, slope_2, tokens.shape[1]).T
        return (token_grad, weight_grad)

    return jax.shard_map(
        on_device,
        mesh=mesh,
        in_specs=(P(AXES, None), P("fsdp", None), P(AXES, None)),
        out_specs=(P(AXES, None), P("fsdp", None)),
        check_vma=False,
    )
```

```python
import jax
import jax.numpy as jnp
from jax import lax
from jax.experimental import pallas as pl
from jax.experimental.pallas import tpu as pltpu
from jax.sharding import PartitionSpec as P

AXES = ("fsdp", "rep")
HOPS = 2
LINE = 16
SPAN = 5
MIB = 1024 * 1024


def _band(near, far, w_own):
    n = near[0].shape[0] // 2
    below = [v[:n] for v in far] + [v[:n] for v in near]
    above = [v[n:] for v in near] + [v[n:] for v in far]
    return jnp.concatenate(below + [w_own[...]] + above, axis=0)


def slope_kernel(with_own, core, tok_a, tok_b, n0, n1, f0, f1, w_own, cot_a, cot_b, p_two, p_one, *rest):
    slope_out, tok_s = rest[-2:]
    rows = w_own.shape[0]
    half = tok_a.shape[1]
    tok_s[:, :half] = tok_a[...]
    tok_s[:, half:] = tok_b[...]
    pre = jnp.dot(tok_s[...].T, _band((n0, n1), (f0, f1), w_own), preferred_element_type=jnp.float32)
    s = 0.5 * jnp.tanh(0.5 * pre) + 0.5
    d = s * (1.0 + pre * (1.0 - s))
    up = jnp.concatenate([cot_a[...], cot_b[...]], axis=0)
    slope = (up.astype(jnp.float32) * d).astype(jnp.bfloat16)
    slope_out[...] = slope[:half]
    two = pl.multiple_of(jnp.where(core[0] == 0, SPAN - 1, 0) * rows, rows)
    one = pl.multiple_of(jnp.where(core[0] == 0, SPAN - 2, 1) * rows, rows)
    blocks = [tok_s[pl.ds(two, rows)], tok_s[pl.ds(one, rows)]]
    if with_own:
        blocks.append(tok_s[HOPS * rows:(HOPS + 1) * rows])
    part = jnp.dot(jnp.concatenate(blocks, axis=0), slope, preferred_element_type=jnp.float32)
    p_two[...] = part[:rows].astype(jnp.bfloat16)
    p_one[...] = part[rows:2 * rows].astype(jnp.bfloat16)
    if with_own:
        rest[0][...] = part[2 * rows:].astype(jnp.bfloat16)


def grad_kernel(core, n0, n1, f0, f1, w_own, s_first, s_second, tg):
    cols = s_first.shape[1]

    def one(first, second):
        band = _band((n0, n1), (f0, f1), w_own)
        total = jnp.zeros(tg.shape, jnp.float32)
        for k, slope in enumerate((first, second)):
            total += lax.dot_general(band[:, k * cols:(k + 1) * cols], slope[...], (((1,), (1,)), ((), ())),
                                     preferred_element_type=jnp.float32)
        tg[...] = total.astype(tg.dtype)

    @pl.when(core[0] == 0)
    def _():
        one(s_second, s_first)

    @pl.when(core[0] != 0)
    def _():
        one(s_first, s_second)


def slopes(core, tok_a, tok_b, pairs, weight, cot_a, cot_b, own_cols):
    width, rows = tok_a.shape
    shard, cols = weight.shape[0], weight.shape[1] // 2
    where = (lambda i, c: (0, c[0])) if own_cols else (lambda i, c: (0, 1 - c[0]))
    whole = lambda v: pl.BlockSpec(v.shape, lambda i, c: (0, 0))
    col = lambda v: pl.BlockSpec((v.shape[0], cols), where)
    out = lambda r: pl.BlockSpec((r, cols), lambda i, c: (0, 0))
    heights = [shard] * (3 if own_cols else 2) + [rows]
    return pl.pallas_call(
        lambda *refs: slope_kernel(own_cols, *refs),
        grid_spec=pltpu.PrefetchScalarGridSpec(
            num_scalar_prefetch=1,
            grid=(1,),
            in_specs=[whole(tok_a), whole(tok_b)] + [col(v) for v in pairs] + [col(weight), col(cot_a), col(cot_b)],
            out_specs=[out(r) for r in heights],
            scratch_shapes=[pltpu.VMEM((width, 2 * rows), jnp.bfloat16)],
        ),
        out_shape=[jax.ShapeDtypeStruct((r, cols), jnp.bfloat16) for r in heights],
        compiler_params=pltpu.CompilerParams(vmem_limit_bytes=40 * MIB),
        cost_estimate=pl.CostEstimate(flops=7 * width * rows * cols, bytes_accessed=6 * MIB,
                                      transcendentals=2 * rows * cols),
    )(core, tok_a, tok_b, *pairs, weight, cot_a, cot_b)


def token_gradient(core, pairs, weight, first, second, width):
    rows = first.shape[0]
    whole = lambda v: pl.BlockSpec(v.shape, lambda i, c: (0, 0))
    return pl.pallas_call(
        grad_kernel,
        grid_spec=pltpu.PrefetchScalarGridSpec(
            num_scalar_prefetch=1,
            grid=(1,),
            in_specs=[whole(v) for v in (*pairs, weight, first, second)],
            out_specs=pl.BlockSpec((width, rows), lambda i, c: (0, 0)),
        ),
        out_shape=jax.ShapeDtypeStruct((width, rows), jnp.bfloat16),
        compiler_params=pltpu.CompilerParams(vmem_limit_bytes=40 * MIB),
        cost_estimate=pl.CostEstimate(flops=4 * width * rows * first.shape[1], bytes_accessed=6 * MIB, transcendentals=0),
    )(core, *pairs, weight, first, second)


def solution(mesh):
    n_f, n_r = mesh.shape["fsdp"], mesh.shape["rep"]

    def pairs_of(move):
        out = []
        for p in range(n_f):
            for r in range(n_r):
                q, t = move(p, r)
                if q != q % n_f:
                    t ^= 2
                out.append((p * n_r + r, (q % n_f) * n_r + t))
        return out

    ring = pairs_of(lambda p, r: (p + (1 if r % 2 == 0 else -1), r))
    crosses = lambda pair: (pair[0] // n_r) // LINE != (pair[1] // n_r) // LINE
    inner = [pair for pair in ring if not crosses(pair)]
    outer = [pair for pair in ring if crosses(pair)]
    swap_core = pairs_of(lambda p, r: (p, r ^ 1))
    far_groups = [[g, g + 2] for g in range(2)]
    core_groups = [[g, g + 1] for g in range(0, n_r, 2)]

    def on_device(tokens, weight, cotangent):
        core = lax.axis_index("rep") % 2
        half = weight.shape[0] // 2

        def send(v, how):
            return lax.ppermute(v, AXES, how)

        def gather(v, axis):
            return lax.all_gather(v, "rep", axis=axis, tiled=True, axis_index_groups=core_groups)

        f32 = lambda v: v.astype(jnp.float32)
        b16 = lambda v: v.astype(jnp.bfloat16)
        step_in = send(weight, inner)
        step_out = send(weight, outer)
        parts = lax.optimization_barrier((step_in[:half], step_in[half:]))
        far_out = [send(v, outer) for v in parts]
        near = [parts[0] + step_out[:half], parts[1] + step_out[half:]]
        far = [send(v, inner) for v in near]
        far = [v + w for v, w in zip(far, far_out)]
        cot_b = send(cotangent, swap_core)
        tok_a = tokens.T
        tok_b = send(tok_a, swap_core)
        pairs = [gather(v, 0) for v in near + far]
        which = core.reshape(1).astype(jnp.int32)
        two, one, slope_1 = slopes(which, tok_a, tok_b, pairs, weight, cotangent, cot_b, False)
        g_1 = send(two, ring)
        two_2, one_2, own, slope_2 = slopes(which, tok_a, tok_b, pairs, weight, cotangent, cot_b, True)
        g_2 = send(two_2, ring)
        g_1 = send(b16(f32(g_1) + f32(one)), ring)
        g_2 = send(b16(f32(g_2) + f32(one_2)), ring)
        got = send(g_1, swap_core)
        mine = b16(f32(own) + f32(g_2) + f32(got))
        both = lax.all_gather(mine, "rep", axis=0, tiled=True, axis_index_groups=far_groups)
        rows = weight.shape[0]
        weight_grad = gather(b16(f32(both[:rows]) + f32(both[rows:])), 1)
        token_grad = token_gradient(which, pairs, weight, slope_1, slope_2, tokens.shape[1]).T
        return (token_grad, weight_grad)

    return jax.shard_map(
        on_device,
        mesh=mesh,
        in_specs=(P(AXES, None), P("fsdp", None), P(AXES, None)),
        out_specs=(P(AXES, None), P("fsdp", None)),
        check_vma=False,
    )
```
